32 devices in a mesh: group: 2 (over x), row: 16 (over z, y, core).
Axes of the slice: x: 2, y: 2, z: 4, core: 2. Of those that a mesh axis runs over, the one named last changes fastest.
Arguments:
- base_currents: bfloat16 [32768, 1024], P(('group', 'row')), parts along dimension 0, may hold values from -6 to 6
- term_rows: bfloat16 [8192, 1024], P(('group', 'row')), parts along dimension 0, may hold values from -12 to 12
- term_owner: int32 [8192, 1], P(('group', 'row')), parts along dimension 0, may hold values from 0 to 15; in each aligned block of 256 rows (0 to 255, 256 to 511, ...) at most 32 rows name the same one
- term_slot: int32 [8192, 1], P(('group', 'row')), parts along dimension 0, may hold values from 0 to 1023
- inductance: bfloat16 [64, 20, 256, 256], P('row'), may hold values from -0.078125 to 0.078125
- block_cols: int32 [64, 20], P('row'), may hold values from 0 to 63, as said below
Outputs:
- flux: bfloat16 [32768, 1024], P(('group', 'row')), parts along dimension 0
The draws below stay inside these ranges and needn't reach their ends.
There are 2 independent parts, one for each index of `group`. The reference program is written for one: setup_inputs(seed, part) draws one part's arguments, and reference() takes and returns one part's arrays. A program takes and returns all parts, laid end to end along the dimension named above; an argument that names none is the same for every part. Nothing has to cross between parts.
Inputs may be any that keep to these rules, and one draw needn't show every extreme that they name: `block_cols`: the block rows of device i (block rows i * 4 to i * 4 + 3) list only block columns of devices i - 2 to i + 2; every block row lists a column of device max(i - 2, 0) and one of device min(i + 2, the last device). Columns may repeat. `term_owner`: among the 256 terminal rows of one device, at most 32 name the same owner, and that many is reached.
All inputs are finite; a program needn't handle non-finite values.
Results may differ from the reference program's by a relative error of at most 0.0046.
Values may be sent and summed in bfloat16 or wider, within the bound.
A program may use at most 128 MiB of HBM per device.

```python
import math
import jax
import jax.numpy as jnp
import numpy as np
from jax import lax

BLOCK = 256
RB_DEV = 4
K = 20
HALO = 2
W = 1024
TERM_DEV = 256
CAP = 32
SEG_DEV = 1024
ORDER = 16384
BROWS = 64
TERMS = 4096
N_ROW = 16


def draw_block_cols(key, part):
    devices = BROWS // RB_DEV
    row_ids = jnp.arange(BROWS)
    home_dev = row_ids // RB_DEV
    lowest = jnp.maximum(home_dev - HALO, 0)
    highest = jnp.minimum(home_dev + HALO, devices - 1)
    key_owner = jax.random.fold_in(key, 11)
    key_within = jax.random.fold_in(key, 12)
    key_forced = jax.random.fold_in(key, 13)
    owner_dev = jax.random.randint(key_owner, (BROWS, K), lowest[:, None], highest[:, None] + 1)
    forced = jax.random.randint(key_forced, (BROWS, 1), 0, K)
    entry_ids = jnp.arange(K)[None, :]
    owner_dev = jnp.where(entry_ids == forced, lowest[:, None], owner_dev)
    owner_dev = jnp.where(entry_ids == (forced + 1) % K, highest[:, None], owner_dev)
    within = jax.random.randint(key_within, (BROWS, K), 0, RB_DEV)
    return (owner_dev * RB_DEV + within).astype(jnp.int32)


def touch_ends(entries, rng, least, top_value):
    index_at = [jax.random.randint(jax.random.fold_in(rng, axis), (), 0, length) for axis, length in enumerate(entries.shape)]
    main_axis = entries.shape.index(max(entries.shape))
    next_to = index_at[:main_axis] + [(index_at[main_axis] + 1) % entries.shape[main_axis]] + index_at[main_axis + 1:]
    return entries.at[tuple(index_at)].set(least).at[tuple(next_to)].set(top_value)


def level_of(key, extent, cuts, least, largest):
    def one(axis_at, parts):
        steps = jax.random.uniform(jax.random.fold_in(jax.random.fold_in(key, 6), axis_at), (parts,), jnp.float32, least / len(cuts), largest / len(cuts))
        return jnp.repeat(jnp.exp(steps), extent[axis_at] // parts).reshape((-1,) + (1,) * (len(extent) - axis_at - 1))

    factor_of = one(*cuts[0])
    for cut in cuts[1:]:
        factor_of = factor_of * one(*cut)
    return factor_of


def routed_block(rng, own, number, rows, count, top, bound, lean):
    order = jax.random.permutation(rng, count)
    heavy_load, usual = portions_of(count, rows * top, bound, lean, True), portions_of(count, rows * top, bound, lean, False)
    places = jnp.arange(count)

    def named(lengths, rotation):
        used = int((lengths > 0).sum())
        fixed = max(1, used // 4)
        shifted = fixed + (places - fixed + rotation * (used - fixed)) % max(1, count - fixed)
        return jnp.zeros((count,), jnp.int32).at[order[jnp.where(places < fixed, places, shifted)]].set(jnp.asarray(lengths, jnp.int32))

    lengths = jnp.where(number % 4 == 0, named(heavy_load, number // 4), named(usual, number - number // 4 - 1))
    mixed = jax.random.permutation(jax.random.fold_in(own, 3), count)
    source_of, taker = mixed[0:count // 2 * 2:2], mixed[1:count // 2 * 2:2]
    margin = jnp.minimum(lengths[source_of] - 1, bound - lengths[taker]) // 2
    margin = jnp.where((source_of == order[0]) | (taker == order[0]) | (lengths[taker] == 0), 0, jnp.maximum(margin, 0))
    shifted = jax.random.randint(jax.random.fold_in(own, 4), (count // 2,), 0, 1 << 20) % (margin + 1)
    lengths = lengths.at[source_of].add(-shifted).at[taker].add(shifted)
    members = jnp.searchsorted(jnp.cumsum(lengths), jnp.arange(rows * top), side="right").astype(jnp.int32)
    grid = members.reshape(top, rows).T
    grid = grid[jax.random.permutation(jax.random.fold_in(own, 1), rows)]
    rotation = jax.random.randint(jax.random.fold_in(own, 2), (rows, 1), 0, top)
    return jnp.take_along_axis(grid, (jnp.arange(top)[None, :] + rotation) % top, axis=1)


def portions_of(number_of, total, bound, skew, full):
    loads = [(1 << 20) // math.isqrt(rank ** skew) + 1 for rank in range(1, number_of + 1)]
    largest = bound if full else min(bound, max(-(-total // number_of), total * loads[0] // sum(loads)))
    least = 1 if total - largest >= number_of - 1 else 0
    counts, spare = [largest] + [least] * (number_of - 1), total - largest - least * (number_of - 1)
    while spare > 0:
        free = [i for i in range(1, number_of) if counts[i] < largest] or [i for i in range(1, number_of) if counts[i] < bound]
        pool, budget = sum([loads[i] for i in free]), spare
        for i in free:
            addition = min(bound - counts[i], max(1, budget * loads[i] // pool), spare)
            counts[i] = counts[i] + addition
            spare = spare - addition
    return np.array(counts)


def bell_draw(key, dims, width, reach, shards=(), kind=jnp.bfloat16):
    array = width * jax.random.normal(key, dims, jnp.float32)
    if shards:
        array = array * level_of(key, dims, shards, -0.22, 0.18)
    return jnp.clip(array, -reach, reach).astype(kind)


def setup_inputs(seed: int = 0, part: int = 0) -> dict:
    splits = jax.random.split(jax.random.key(seed), 7)
    own_keys = jax.random.split(jax.random.fold_in(splits[6], part), 7)
    base_currents = bell_draw(own_keys[0], (ORDER, W), 1.0, 6.0, ((0, 16),))
    term_rows = bell_draw(own_keys[1], (TERMS, W), 3.0, 12.0, ((0, 16),))
    term_owner_keys = jax.random.split(jax.random.fold_in(own_keys[2], 1), TERMS // TERM_DEV)
    term_owner_turns = jax.random.permutation(jax.random.fold_in(own_keys[2], 3), TERMS // TERM_DEV)
    term_owner = jax.vmap(lambda own, number: routed_block(jax.random.fold_in(own_keys[2], 2), own, number, TERM_DEV, N_ROW, 1, CAP, 2))(term_owner_keys, term_owner_turns).reshape((TERMS, 1))
    term_slot = touch_ends(jax.random.randint(own_keys[3], (TERMS, 1), 0, SEG_DEV), jax.random.fold_in(own_keys[3], 1), 0, SEG_DEV - 1).astype(jnp.int32)
    inductance = bell_draw(splits[4], (BROWS, K, BLOCK, BLOCK), (K * BLOCK) ** -0.5, 0.078125, ((0, 16),))
    block_cols = draw_block_cols(jax.random.fold_in(splits[6], 71), part)
    return {"base_currents": base_currents, "term_rows": term_rows, "term_owner": term_owner, "term_slot": term_slot, "inductance": inductance, "block_cols": block_cols}


def reference(base_currents, term_rows, term_owner, term_slot, inductance, block_cols):
    segment_of = (term_owner[:, 0] * SEG_DEV + term_slot[:, 0]).astype(jnp.int32)
    injected = jax.ops.segment_sum(term_rows.astype(jnp.float32), segment_of, num_segments=ORDER)
    currents = (base_currents.astype(jnp.float32) + injected).astype(jnp.bfloat16)
    current_blocks = currents.reshape(BROWS, BLOCK, W)

    def one_row(inputs):
        tiles, columns = inputs
        picked = current_blocks[columns.astype(jnp.int32)]
        return jnp.einsum("kab,kbw->aw", tiles.astype(jnp.float32), picked.astype(jnp.float32))

    linked = lax.map(one_row, (inductance, block_cols))
    return linked.reshape(ORDER, W).astype(jnp.bfloat16)
```

```python
import functools

import jax
import jax.numpy as jnp
from jax import lax
from jax.experimental import pallas as pl
from jax.experimental.pallas import tpu as pltpu
from jax.sharding import PartitionSpec as P

CHUNKS = 4
LANES = 128
HALO = 2
MESH = pl.DeviceIdType.MESH
F32 = jnp.float32
BF16 = jnp.bfloat16
TO_Y, TO_Z, TO_CORE, TO_RELAY = range(4)


def kernel(n, cap, cols_ref, owner_ref, slot_ref, terms_hbm, base_hbm, blocks_hbm, out_hbm, *scratch):
    windows, scratch = scratch[:CHUNKS], scratch[CHUNKS:]
    outgoing, scratch = scratch[:CHUNKS], scratch[CHUNKS:]
    arrived, scratch = scratch[:CHUNKS], scratch[CHUNKS:]
    results, scratch = scratch[:CHUNKS], scratch[CHUNKS:]
    (terms, base, blocks, landing, tags_out, tags_in,
     load_sem, own_sem, store_sem, a2a_send, a2a_recv, tag_send, tag_recv, halo_send, halo_recv) = scratch
    me = lax.axis_index("row")
    count = terms.shape[0]
    seg_dev = base.shape[0]
    rows_dev, stored, block, _ = blocks.shape
    wide = windows[0].shape[2]
    sign_c = 1 - 2 * (me % 2)
    sign_y = 1 - 2 * ((me // 2) % 2)
    z_to, z_from = me + 4 * sign_y, me - 4 * sign_y
    z_sends = jnp.logical_and(z_to >= 0, z_to < n)
    z_comes = jnp.logical_and(z_from >= 0, z_from < n)

    load_terms = pltpu.make_async_copy(terms_hbm, terms, load_sem.at[0])
    load_base = pltpu.make_async_copy(base_hbm, base, load_sem.at[1])
    load_blocks = pltpu.make_async_copy(blocks_hbm, blocks, load_sem.at[2])
    load_terms.start()
    load_base.start()
    load_blocks.start()

    barrier = pltpu.get_barrier_semaphore()

    @pl.loop(1, n)
    def _(step):
        pl.semaphore_signal(barrier, inc=1, device_id={"row": (me + step) % n}, device_id_type=MESH)

    owner = owner_ref[...]
    matches = (lax.broadcasted_iota(jnp.int32, (n, count), 0) == owner).astype(F32)
    before = lax.broadcasted_iota(jnp.int32, (count, count), 0) < lax.broadcasted_iota(jnp.int32, (count, count), 1)
    earlier = jnp.dot(matches.astype(BF16), before.astype(F32).astype(BF16), preferred_element_type=F32)
    order_in = jnp.sum(earlier * matches, axis=0, keepdims=True).astype(jnp.int32)
    position = owner * cap + order_in
    picker = (lax.broadcasted_iota(jnp.int32, (n * cap, count), 0) == position).astype(F32).astype(BF16)
    per_row = LANES // cap
    lane_of = order_in + (me % per_row) * cap
    lanes = (lax.broadcasted_iota(jnp.int32, (LANES, count), 0) == lane_of).astype(F32).astype(BF16)
    tag = slot_ref[...] + 1
    high = (tag // 32).astype(F32)
    low = (tag % 32).astype(F32)
    over_rows = (((1,), (1,)), ((), ()))
    tags = 32.0 * lax.dot_general((matches * high).astype(BF16), lanes, over_rows, preferred_element_type=F32)
    tags = tags + lax.dot_general((matches * low).astype(BF16), lanes, over_rows, preferred_element_type=F32)
    tags = tags.astype(jnp.int32)
    for peer in range(n):
        tags_out[peer] = jnp.broadcast_to(tags[peer:peer + 1], tags_out.shape[1:])

    def tag_copy(peer, source):
        return pltpu.make_async_remote_copy(
            src_ref=tags_out.at[peer], dst_ref=tags_in.at[source], send_sem=tag_send.at[peer],
            recv_sem=tag_recv.at[source], device_id={"row": peer}, device_id_type=MESH)

    def row_copy(j, peer, source):
        return pltpu.make_async_remote_copy(
            src_ref=outgoing[j].at[peer], dst_ref=arrived[j].at[source], send_sem=a2a_send.at[j, peer],
            recv_sem=a2a_recv.at[j, source], device_id={"row": peer}, device_id_type=MESH)

    load_terms.wait()
    pl.semaphore_wait(barrier, n - 1)

    @pl.loop(1, n)
    def _(step):
        tag_copy((me + step) % n, me).start()

    own_tags = pltpu.make_async_copy(tags_out.at[me], tags_in.at[me], own_sem.at[CHUNKS])
    own_tags.start()
    own_rows = []
    for j in range(CHUNKS):
        sent = jnp.dot(picker, terms[:, j * wide:(j + 1) * wide], preferred_element_type=F32)
        outgoing[j][...] = sent.astype(BF16).reshape(outgoing[j].shape)

        @pl.loop(1, n)
        def _(step):
            row_copy(j, (me + step) % n, me).start()

        own_rows.append(pltpu.make_async_copy(outgoing[j].at[me], arrived[j].at[me], own_sem.at[j]))
        own_rows[-1].start()

    @pl.loop(1, n)
    def _(step):
        source = (me + step) % n
        tag_copy(source, source).wait_recv()

    own_tags.wait()
    packed = []
    for first in range(0, n, per_row):
        total = tags_in[first][0:1]
        for source in range(first + 1, min(first + per_row, n)):
            total = total + tags_in[source][0:1]
        packed.append(total)
    arrived_tags = jnp.concatenate(packed, axis=1) - 1
    tall = seg_dev // 4
    for part in range(4):
        seg_ids = lax.broadcasted_iota(jnp.int32, (tall, n * cap), 0) + part * tall
        landing[part * tall:(part + 1) * tall] = (seg_ids == arrived_tags).astype(F32).astype(BF16)
    load_base.wait()

    def halo_copy(kind, j, from_slot, to_slot, peer):
        return pltpu.make_async_remote_copy(
            src_ref=windows[j].at[pl.ds(rows_dev * from_slot, rows_dev)],
            dst_ref=windows[j].at[pl.ds(rows_dev * to_slot, rows_dev)],
            send_sem=halo_send.at[kind, j], recv_sem=halo_recv.at[kind, j],
            device_id={"row": peer}, device_id_type=MESH)

    def y_send(j):
        return halo_copy(TO_Y, j, HALO, HALO - 2 * sign_y, me + 2 * sign_y)

    def core_send(j):
        return halo_copy(TO_CORE, j, HALO, HALO - sign_c, me + sign_c)

    def z_send(j):
        return halo_copy(TO_Z, j, HALO + 2 * sign_y, HALO - 2 * sign_y, z_to)

    def relay_send(j):
        return halo_copy(TO_RELAY, j, HALO + 2 * sign_c, HALO + sign_c, me + sign_c)

    def wait_for(kind, j, slot, peer):
        halo_copy(kind, j, slot, slot, peer).wait_recv()

    def own(j):
        @pl.loop(1, n)
        def _(step):
            source = (me + step) % n
            row_copy(j, source, source).wait_recv()

        own_rows[j].wait()
        rows = arrived[j][...].reshape(n * cap, wide)
        for part in range(seg_dev // block):
            place = slice(part * block, (part + 1) * block)
            injected = jnp.dot(landing[place], rows, preferred_element_type=F32)
            before_it = base[place, j * wide:(j + 1) * wide].astype(F32)
            windows[j][HALO * rows_dev + part] = (before_it + injected).astype(BF16)
        y_send(j).start()
        core_send(j).start()

    def y_arrives(j):
        wait_for(TO_Y, j, HALO + 2 * sign_y, me + 2 * sign_y)

        @pl.when(z_sends)
        def _():
            z_send(j).start()

        @pl.when(sign_y == sign_c)
        def _():
            relay_send(j).start()

    def z_arrives(j):
        @pl.when(z_comes)
        def _():
            wait_for(TO_Z, j, HALO - 2 * sign_y, me + 2 * sign_y)

        @pl.when(jnp.logical_and(z_comes, sign_y != sign_c))
        def _():
            relay_send(j).start()

    relay_sends = jnp.logical_or(sign_y == sign_c, z_comes)
    relay_comes = jnp.logical_or(sign_y != sign_c, z_comes)
    first_block = (me - HALO) * rows_dev

    def compute(j):
        wait_for(TO_CORE, j, HALO + sign_c, me + sign_c)

        @pl.when(relay_comes)
        def _():
            wait_for(TO_RELAY, j, HALO - sign_c, me + sign_c)

        @pl.loop(0, rows_dev)
        def _(r):
            total = jnp.zeros((block, wide), F32)
            for k in range(stored):
                place = jnp.clip(cols_ref[r, k] - first_block, 0, windows[j].shape[0] - 1)
                picked = windows[j][place]
                total = total + jnp.dot(blocks[r, k], picked, preferred_element_type=F32)
            results[j][pl.ds(pl.multiple_of(r * block, block), block)] = total.astype(BF16)

        store(j).start()

    def store(j):
        return pltpu.make_async_copy(results[j], out_hbm.at[:, pl.ds(j * wide, wide)], store_sem.at[j])

    own(0)
    own(1)
    for j in range(CHUNKS):
        y_arrives(j)
        if j + 2 < CHUNKS:
            own(j + 2)
        if j == 0:
            load_blocks.wait()
        else:
            z_arrives(j - 1)
            compute(j - 1)
    z_arrives(CHUNKS - 1)
    compute(CHUNKS - 1)

    @pl.loop(1, n)
    def _(step):
        peer = (me + step) % n
        tag_copy(peer, me).wait_send()
        for j in range(CHUNKS):
            row_copy(j, peer, me).wait_send()

    for j in range(CHUNKS):
        y_send(j).wait_send()
        core_send(j).wait_send()

        @pl.when(z_sends)
        def _():
            z_send(j).wait_send()

        @pl.when(relay_sends)
        def _():
            relay_send(j).wait_send()

        store(j).wait()


def shards(base_currents, term_rows, term_owner, term_slot, inductance, block_cols):
    n = lax.axis_size("row")
    seg_dev, width = base_currents.shape
    count = term_rows.shape[0]
    rows_dev, stored, block, _ = inductance.shape
    cap = max(16, 2 * count // n)
    wide = width // CHUNKS
    span = (2 * HALO + 1) * rows_dev
    vmem = pl.BlockSpec(memory_space=pltpu.VMEM)
    smem = pl.BlockSpec(memory_space=pltpu.SMEM)
    hbm = pl.BlockSpec(memory_space=pl.ANY)
    dma = pltpu.SemaphoreType.DMA
    return pl.pallas_call(
        functools.partial(kernel, n, cap),
        out_shape=jax.ShapeDtypeStruct((seg_dev, width), BF16),
        in_specs=[smem, vmem, vmem, hbm, hbm, hbm],
        out_specs=hbm,
        scratch_shapes=(
            [pltpu.VMEM((span, block, wide), BF16)] * CHUNKS
            + [pltpu.VMEM((n, cap, wide), BF16)] * CHUNKS
            + [pltpu.VMEM((n, cap, wide), BF16)] * CHUNKS
            + [pltpu.VMEM((seg_dev, wide), BF16)] * CHUNKS
            + [
                pltpu.VMEM((count, width), BF16),
                pltpu.VMEM((seg_dev, width), BF16),
                pltpu.VMEM(inductance.shape, BF16),
                pltpu.VMEM((seg_dev, n * cap), BF16),
                pltpu.VMEM((n, 8, LANES), jnp.int32),
                pltpu.VMEM((n, 8, LANES), jnp.int32),
                dma((3,)),
                dma((CHUNKS + 1,)),
                dma((CHUNKS,)),
                dma((CHUNKS, n)),
                dma((CHUNKS, n)),
                dma((n,)),
                dma((n,)),
                dma((4, CHUNKS)),
                dma((4, CHUNKS)),
            ]
        ),
        compiler_params=pltpu.CompilerParams(
            collective_id=0, has_side_effects=True, vmem_limit_bytes=50 * 2**20
        ),
        cost_estimate=pl.CostEstimate(
            flops=2 * rows_dev * stored * block * block * width,
            bytes_accessed=2 * (inductance.size + 2 * base_currents.size + term_rows.size),
            transcendentals=0,
        ),
    )(block_cols, term_owner.reshape(1, count), term_slot.reshape(1, count), term_rows, base_currents, inductance)


def solution(mesh):
    placed = (
        P(("group", "row"), None),
        P(("group", "row"), None),
        P(("group", "row"), None),
        P(("group", "row"), None),
        P("row", None, None, None),
        P("row", None),
    )
    return jax.shard_map(
        shards, mesh=mesh, in_specs=placed, out_specs=P(("group", "row"), None), check_vma=False
    )
```

```python
import functools

import jax
import jax.numpy as jnp
from jax import lax
from jax.experimental import pallas as pl
from jax.experimental.pallas import tpu as pltpu
from jax.sharding import PartitionSpec as P

CHUNKS = 4
LANES = 128
HALO = 2
MESH = pl.DeviceIdType.MESH
F32 = jnp.float32
BF16 = jnp.bfloat16
TO_Y, TO_Z, TO_CORE, TO_RELAY = range(4)


def kernel(n, cap, cols_hbm, owner_hbm, slot_hbm, terms_hbm, base_hbm, blocks_hbm, out_hbm, *scratch):
    windows, scratch = scratch[:CHUNKS], scratch[CHUNKS:]
    outgoing, scratch = scratch[:CHUNKS], scratch[CHUNKS:]
    arrived, scratch = scratch[:CHUNKS], scratch[CHUNKS:]
    results, scratch = scratch[:CHUNKS], scratch[CHUNKS:]
    (cols_ref, owner_ref, slot_ref, terms, base, blocks, landing, tags_out, tags_in,
     load_sem, own_sem, store_sem, a2a_send, a2a_recv, tag_sem, halo_send, halo_recv, piece_recv) = scratch
    me = lax.axis_index("row")
    count = terms.shape[0]
    seg_dev = base.shape[0]
    rows_dev, stored, block, _ = blocks.shape
    wide = windows[0].shape[2]
    sign_c = 1 - 2 * (me % 2)
    sign_y = 1 - 2 * ((me // 2) % 2)
    z_to, z_from = me + 4 * sign_y, me - 4 * sign_y
    z_sends = jnp.logical_and(z_to >= 0, z_to < n)
    z_comes = jnp.logical_and(z_from >= 0, z_from < n)

    load_terms = pltpu.make_async_copy(terms_hbm, terms, load_sem.at[0])
    load_base = pltpu.make_async_copy(base_hbm, base, load_sem.at[1])
    load_blocks = pltpu.make_async_copy(blocks_hbm, blocks, load_sem.at[2])
    load_owner = pltpu.make_async_copy(owner_hbm, owner_ref, load_sem.at[3])
    load_slot = pltpu.make_async_copy(slot_hbm, slot_ref, load_sem.at[4])
    load_cols = pltpu.make_async_copy(cols_hbm, cols_ref, load_sem.at[5])
    for load in (load_owner, load_slot, load_terms, load_base, load_cols, load_blocks):
        load.start()

    barrier = pltpu.get_barrier_semaphore()

    @pl.loop(1, n)
    def _(step):
        pl.semaphore_signal(barrier, inc=1, device_id={"row": (me + step) % n}, device_id_type=MESH)

    load_owner.wait()
    owner = owner_ref[...]
    matches = (lax.broadcasted_iota(jnp.int32, (n, count), 0) == owner).astype(F32)
    before = lax.broadcasted_iota(jnp.int32, (count, count), 0) < lax.broadcasted_iota(jnp.int32, (count, count), 1)
    earlier = jnp.dot(matches.astype(BF16), before.astype(F32).astype(BF16), preferred_element_type=F32)
    order_in = jnp.sum(earlier * matches, axis=0, keepdims=True).astype(jnp.int32)
    position = owner * cap + order_in
    picker = (lax.broadcasted_iota(jnp.int32, (n * cap, count), 0) == position).astype(F32).astype(BF16)
    def tag_copy(peer, source):
        return pltpu.make_async_remote_copy(
            src_ref=tags_out.at[peer], dst_ref=tags_in.at[source], send_sem=tag_sem.at[0],
            recv_sem=tag_sem.at[1], device_id={"row": peer}, device_id_type=MESH)

    def row_copy(j, peer, source):
        return pltpu.make_async_remote_copy(
            src_ref=outgoing[j].at[peer], dst_ref=arrived[j].at[source], send_sem=a2a_send.at[j],
            recv_sem=a2a_recv.at[j], device_id={"row": peer}, device_id_type=MESH)

    def all_tags():
        others = pl.ds(0, n - 1)
        return pltpu.make_async_remote_copy(
            src_ref=tags_out.at[others], dst_ref=tags_in.at[others], send_sem=tag_sem.at[0],
            recv_sem=tag_sem.at[1], device_id={"row": (me + 1) % n}, device_id_type=MESH)

    def all_rows(j):
        others = pl.ds(0, n - 1)
        return pltpu.make_async_remote_copy(
            src_ref=outgoing[j].at[others], dst_ref=arrived[j].at[others], send_sem=a2a_send.at[j],
            recv_sem=a2a_recv.at[j], device_id={"row": (me + 1) % n}, device_id_type=MESH)

    own_tags = pltpu.make_async_copy(tags_out.at[me], tags_in.at[me], own_sem.at[CHUNKS])
    own_rows = [
        pltpu.make_async_copy(outgoing[j].at[me], arrived[j].at[me], own_sem.at[j]) for j in range(CHUNKS)
    ]

    def pack(j):
        sent = jnp.dot(picker, terms[:, j * wide:(j + 1) * wide], preferred_element_type=F32)
        outgoing[j][...] = sent.astype(BF16).reshape(outgoing[j].shape)

    def send_rows(j):
        @pl.loop(1, n)
        def _(step):
            row_copy(j, (me + step) % n, me).start()

        own_rows[j].start()

    load_terms.wait()
    pack(0)
    pl.semaphore_wait(barrier, n - 1)
    send_rows(0)
    per_row = LANES // cap
    lane_of = order_in + (me % per_row) * cap
    lanes = (lax.broadcasted_iota(jnp.int32, (LANES, count), 0) == lane_of).astype(F32).astype(BF16)
    load_slot.wait()
    tag = slot_ref[...] + 1
    high = (tag // 32).astype(F32)
    low = (tag % 32).astype(F32)
    over_rows = (((1,), (1,)), ((), ()))
    tags = 32.0 * lax.dot_general((matches * high).astype(BF16), lanes, over_rows, preferred_element_type=F32)
    tags = tags + lax.dot_general((matches * low).astype(BF16), lanes, over_rows, preferred_element_type=F32)
    tags = tags.astype(jnp.int32)
    for peer in range(n):
        tags_out[peer] = jnp.broadcast_to(tags[peer:peer + 1], tags_out.shape[1:])


    @pl.loop(1, n)
    def _(step):
        tag_copy((me + step) % n, me).start()

    own_tags.start()
    for j in range(1, CHUNKS):
        pack(j)
        send_rows(j)

    all_tags().wait_recv()
    own_tags.wait()
    packed = []
    for first in range(0, n, per_row):
        total = tags_in[first][0:1]
        for source in range(first + 1, min(first + per_row, n)):
            total = total + tags_in[source][0:1]
        packed.append(total)
    arrived_tags = jnp.concatenate(packed, axis=1) - 1
    tall = seg_dev // 4
    for part in range(4):
        seg_ids = lax.broadcasted_iota(jnp.int32, (tall, n * cap), 0) + part * tall
        landing[part * tall:(part + 1) * tall] = (seg_ids == arrived_tags).astype(F32).astype(BF16)
    load_base.wait()

    def halo_copy(kind, j, from_slot, to_slot, peer):
        return pltpu.make_async_remote_copy(
            src_ref=windows[j].at[pl.ds(rows_dev * from_slot, rows_dev)],
            dst_ref=windows[j].at[pl.ds(rows_dev * to_slot, rows_dev)],
            send_sem=halo_send.at[kind, j], recv_sem=halo_recv.at[kind, j],
            device_id={"row": peer}, device_id_type=MESH)

    def piece_copy(kind, p, from_slot, to_slot, peer):
        j, q = divmod(p, rows_dev)
        recv_sem = halo_recv.at[kind, j] if kind == TO_RELAY else piece_recv.at[kind, p]
        return pltpu.make_async_remote_copy(
            src_ref=windows[j].at[rows_dev * from_slot + q], dst_ref=windows[j].at[rows_dev * to_slot + q],
            send_sem=halo_send.at[kind, j], recv_sem=recv_sem, device_id={"row": peer}, device_id_type=MESH)

    y_way = (HALO, HALO - 2 * sign_y, me + 2 * sign_y)
    core_way = (HALO, HALO - sign_c, me + sign_c)
    z_way = (HALO + 2 * sign_y, HALO - 2 * sign_y, z_to)
    relay_way = (HALO + 2 * sign_c, HALO + sign_c, me + sign_c)
    relay_sends = jnp.logical_or(sign_y == sign_c, z_comes)
    relay_comes = jnp.logical_or(sign_y != sign_c, z_comes)
    first_block = (me - HALO) * rows_dev
    pieces = CHUNKS * rows_dev

    def own(j):
        all_rows(j).wait_recv()
        own_rows[j].wait()
        rows = arrived[j][...].reshape(n * cap, wide)
        for q in range(rows_dev):
            place = slice(q * block, (q + 1) * block)
            injected = jnp.dot(landing[place], rows, preferred_element_type=F32)
            before_it = base[place, j * wide:(j + 1) * wide].astype(F32)
            windows[j][HALO * rows_dev + q] = (before_it + injected).astype(BF16)
            piece_copy(TO_Y, j * rows_dev + q, *y_way).start()
        halo_copy(TO_CORE, j, *core_way).start()

    def y_arrives(p):
        slot = HALO + 2 * sign_y
        piece_copy(TO_Y, p, slot, slot, me + 2 * sign_y).wait_recv()

        @pl.when(z_sends)
        def _():
            piece_copy(TO_Z, p, *z_way).start()

        @pl.when(sign_y == sign_c)
        def _():
            piece_copy(TO_RELAY, p, *relay_way).start()

    def z_arrives(p):
        slot = HALO - 2 * sign_y

        @pl.when(z_comes)
        def _():
            piece_copy(TO_Z, p, slot, slot, me + 2 * sign_y).wait_recv()

        @pl.when(jnp.logical_and(z_comes, sign_y != sign_c))
        def _():
            piece_copy(TO_RELAY, p, *relay_way).start()

    def window_complete(j):
        halo_copy(TO_CORE, j, HALO + sign_c, HALO + sign_c, me + sign_c).wait_recv()

        @pl.when(relay_comes)
        def _():
            halo_copy(TO_RELAY, j, HALO - sign_c, HALO - sign_c, me + sign_c).wait_recv()

    def compute(j, r):
        total = jnp.zeros((block, wide), F32)
        for k in range(stored):
            place = jnp.clip(cols_ref[r, k] - first_block, 0, windows[j].shape[0] - 1)
            total = total + jnp.dot(blocks[r, k], windows[j][place], preferred_element_type=F32)
        results[j][r * block:(r + 1) * block] = total.astype(BF16)

    def store(j):
        return pltpu.make_async_copy(results[j], out_hbm.at[:, pl.ds(j * wide, wide)], store_sem.at[j])

    own(0)
    own(1)
    z_lag, lag = 2, rows_dev + 2
    for p in range(pieces + lag):
        if p < pieces:
            y_arrives(p)
            if p % rows_dev == 0 and p // rows_dev + 2 < CHUNKS:
                own(p // rows_dev + 2)
        if 0 <= p - z_lag < pieces:
            z_arrives(p - z_lag)
        if p == lag:
            load_cols.wait()
            load_blocks.wait()
            all_tags().wait_send()
            for j in range(CHUNKS):
                all_rows(j).wait_send()
        if p >= lag:
            j, r = divmod(p - lag, rows_dev)
            if r == 0:
                window_complete(j)
            compute(j, r)
            if r == rows_dev - 1:
                store(j).start()

    for j in range(CHUNKS):
        halo_copy(TO_Y, j, *y_way).wait_send()
        halo_copy(TO_CORE, j, *core_way).wait_send()

        @pl.when(z_sends)
        def _():
            halo_copy(TO_Z, j, *z_way).wait_send()

        @pl.when(relay_sends)
        def _():
            halo_copy(TO_RELAY, j, *relay_way).wait_send()

        store(j).wait()


def shards(base_currents, term_rows, term_owner, term_slot, inductance, block_cols):
    n = lax.axis_size("row")
    seg_dev, width = base_currents.shape
    count = term_rows.shape[0]
    rows_dev, stored, block, _ = inductance.shape
    cap = max(16, 2 * count // n)
    wide = width // CHUNKS
    span = (2 * HALO + 1) * rows_dev
    hbm = pl.BlockSpec(memory_space=pl.ANY)
    dma = pltpu.SemaphoreType.DMA
    return pl.pallas_call(
        functools.partial(kernel, n, cap),
        out_shape=jax.ShapeDtypeStruct((seg_dev, width), BF16),
        in_specs=[hbm] * 6,
        out_specs=hbm,
        scratch_shapes=(
            [pltpu.VMEM((span, block, wide), BF16)] * CHUNKS
            + [pltpu.VMEM((n, cap, wide), BF16)] * CHUNKS
            + [pltpu.VMEM((n, cap, wide), BF16)] * CHUNKS
            + [pltpu.VMEM((seg_dev, wide), BF16)] * CHUNKS
            + [
                pltpu.SMEM(block_cols.shape, jnp.int32),
                pltpu.VMEM((1, count), jnp.int32),
                pltpu.VMEM((1, count), jnp.int32),
                pltpu.VMEM((count, width), BF16),
                pltpu.VMEM((seg_dev, width), BF16),
                pltpu.VMEM(inductance.shape, BF16),
                pltpu.VMEM((seg_dev, n * cap), BF16),
                pltpu.VMEM((n, 8, LANES), jnp.int32),
                pltpu.VMEM((n, 8, LANES), jnp.int32),
                dma((6,)),
                dma((CHUNKS + 1,)),
                dma((CHUNKS,)),
                dma((CHUNKS,)),
                dma((CHUNKS,)),
                dma((2,)),
                dma((4, CHUNKS)),
                dma((4, CHUNKS)),
                dma((2, CHUNKS * rows_dev)),
            ]
        ),
        compiler_params=pltpu.CompilerParams(
            collective_id=0, has_side_effects=True, vmem_limit_bytes=60 * 2**20
        ),
        cost_estimate=pl.CostEstimate(
            flops=2 * rows_dev * stored * block * block * width,
            bytes_accessed=2 * (inductance.size + 2 * base_currents.size + term_rows.size),
            transcendentals=0,
        ),
    )(block_cols, term_owner.reshape(1, count), term_slot.reshape(1, count), term_rows, base_currents, inductance)


def solution(mesh):
    placed = (
        P(("group", "row"), None),
        P(("group", "row"), None),
        P(("group", "row"), None),
        P(("group", "row"), None),
        P("row", None, None, None),
        P("row", None),
    )
    return jax.shard_map(
        shards, mesh=mesh, in_specs=placed, out_specs=P(("group", "row"), None), check_vma=False
    )
```

```python
import functools

import jax
import jax.numpy as jnp
from jax import lax
from jax.experimental import pallas as pl
from jax.experimental.pallas import tpu as pltpu
from jax.sharding import PartitionSpec as P

CHUNKS = 4
LANES = 128
HALO = 2
MESH = pl.DeviceIdType.MESH
F32 = jnp.float32
BF16 = jnp.bfloat16
TO_Y, TO_Z, TO_CORE, TO_RELAY = range(4)


def kernel(n, cap, cols_hbm, owner_hbm, slot_hbm, terms_hbm, base_hbm, blocks_hbm, out_hbm, *scratch):
    windows, scratch = scratch[:CHUNKS], scratch[CHUNKS:]
    outgoing, scratch = scratch[:CHUNKS], scratch[CHUNKS:]
    arrived, scratch = scratch[:CHUNKS], scratch[CHUNKS:]
    results, scratch = scratch[:CHUNKS], scratch[CHUNKS:]
    (cols_ref, owner_ref, slot_ref, terms, base, blocks, landing, tags_out, tags_in,
     load_sem, own_sem, store_sem, a2a_send, a2a_recv, tag_sem, halo_send, halo_recv, piece_recv) = scratch
    me = lax.axis_index("row")
    count = terms.shape[0]
    seg_dev = base.shape[0]
    rows_dev, stored, block, _ = blocks.shape
    wide = windows[0].shape[2]
    sign_c = 1 - 2 * (me % 2)
    sign_y = 1 - 2 * ((me // 2) % 2)
    z_to, z_from = me + 4 * sign_y, me - 4 * sign_y
    z_sends = jnp.logical_and(z_to >= 0, z_to < n)
    z_comes = jnp.logical_and(z_from >= 0, z_from < n)

    load_terms = pltpu.make_async_copy(terms_hbm, terms, load_sem.at[0])
    load_base = pltpu.make_async_copy(base_hbm, base, load_sem.at[1])
    load_blocks = pltpu.make_async_copy(blocks_hbm, blocks, load_sem.at[2])
    load_owner = pltpu.make_async_copy(owner_hbm, owner_ref, load_sem.at[3])
    load_slot = pltpu.make_async_copy(slot_hbm, slot_ref, load_sem.at[4])
    load_cols = pltpu.make_async_copy(cols_hbm, cols_ref, load_sem.at[5])
    for load in (load_owner, load_slot, load_terms, load_base, load_cols, load_blocks):
        load.start()

    barrier = pltpu.get_barrier_semaphore()

    @pl.loop(1, n)
    def _(step):
        pl.semaphore_signal(barrier, inc=1, device_id={"row": (me + step) % n}, device_id_type=MESH)

    load_owner.wait()
    owner = owner_ref[...]
    matches = (lax.broadcasted_iota(jnp.int32, (n, count), 0) == owner).astype(F32)
    before = lax.broadcasted_iota(jnp.int32, (count, count), 0) < lax.broadcasted_iota(jnp.int32, (count, count), 1)
    earlier = jnp.dot(matches.astype(BF16), before.astype(F32).astype(BF16), preferred_element_type=F32)
    order_in = jnp.sum(earlier * matches, axis=0, keepdims=True).astype(jnp.int32)
    position = owner * cap + order_in
    picker = (lax.broadcasted_iota(jnp.int32, (n * cap, count), 0) == position).astype(F32).astype(BF16)
    def tag_copy(peer, source):
        return pltpu.make_async_remote_copy(
            src_ref=tags_out.at[peer], dst_ref=tags_in.at[source], send_sem=tag_sem.at[0],
            recv_sem=tag_sem.at[1], device_id={"row": peer}, device_id_type=MESH)

    def row_copy(j, peer, source):
        return pltpu.make_async_remote_copy(
            src_ref=outgoing[j].at[peer], dst_ref=arrived[j].at[source], send_sem=a2a_send.at[j],
            recv_sem=a2a_recv.at[j], device_id={"row": peer}, device_id_type=MESH)

    def all_tags():
        others = pl.ds(0, n - 1)
        return pltpu.make_async_remote_copy(
            src_ref=tags_out.at[others], dst_ref=tags_in.at[others], send_sem=tag_sem.at[0],
            recv_sem=tag_sem.at[1], device_id={"row": (me + 1) % n}, device_id_type=MESH)

    def all_rows(j):
        others = pl.ds(0, n - 1)
        return pltpu.make_async_remote_copy(
            src_ref=outgoing[j].at[others], dst_ref=arrived[j].at[others], send_sem=a2a_send.at[j],
            recv_sem=a2a_recv.at[j], device_id={"row": (me + 1) % n}, device_id_type=MESH)

    own_tags = pltpu.make_async_copy(tags_out.at[me], tags_in.at[me], own_sem.at[CHUNKS])
    own_rows = [
        pltpu.make_async_copy(outgoing[j].at[me], arrived[j].at[me], own_sem.at[j]) for j in range(CHUNKS)
    ]

    def pack(j):
        sent = jnp.dot(picker, terms[:, j * wide:(j + 1) * wide], preferred_element_type=F32)
        outgoing[j][...] = sent.astype(BF16).reshape(outgoing[j].shape)

    def send_rows(j):
        @pl.loop(1, n)
        def _(step):
            row_copy(j, (me + step) % n, me).start()

        own_rows[j].start()

    load_terms.wait()
    pack(0)
    pl.semaphore_wait(barrier, n - 1)
    send_rows(0)
    per_row = LANES // cap
    lane_of = order_in + (me % per_row) * cap
    lanes = (lax.broadcasted_iota(jnp.int32, (LANES, count), 0) == lane_of).astype(F32).astype(BF16)
    load_slot.wait()
    tag = slot_ref[...] + 1
    high = (tag // 32).astype(F32)
    low = (tag % 32).astype(F32)
    over_rows = (((1,), (1,)), ((), ()))
    tags = 32.0 * lax.dot_general((matches * high).astype(BF16), lanes, over_rows, preferred_element_type=F32)
    tags = tags + lax.dot_general((matches * low).astype(BF16), lanes, over_rows, preferred_element_type=F32)
    tags = tags.astype(jnp.int32)
    for peer in range(n):
        tags_out[peer] = jnp.broadcast_to(tags[peer:peer + 1], tags_out.shape[1:])


    @pl.loop(1, n)
    def _(step):
        tag_copy((me + step) % n, me).start()

    own_tags.start()

    def next_rows(j):
        pack(j)
        all_rows(j - 1).wait_send()
        send_rows(j)

    next_rows(1)

    all_tags().wait_recv()
    own_tags.wait()
    packed = []
    for first in range(0, n, per_row):
        total = tags_in[first][0:1]
        for source in range(first + 1, min(first + per_row, n)):
            total = total + tags_in[source][0:1]
        packed.append(total)
    arrived_tags = jnp.concatenate(packed, axis=1) - 1
    tall = seg_dev // 4
    for part in range(4):
        seg_ids = lax.broadcasted_iota(jnp.int32, (tall, n * cap), 0) + part * tall
        landing[part * tall:(part + 1) * tall] = (seg_ids == arrived_tags).astype(F32).astype(BF16)
    load_base.wait()

    def halo_copy(kind, j, from_slot, to_slot, peer):
        return pltpu.make_async_remote_copy(
            src_ref=windows[j].at[pl.ds(rows_dev * from_slot, rows_dev)],
            dst_ref=windows[j].at[pl.ds(rows_dev * to_slot, rows_dev)],
            send_sem=halo_send.at[kind, j], recv_sem=halo_recv.at[kind, j],
            device_id={"row": peer}, device_id_type=MESH)

    def piece_copy(kind, p, from_slot, to_slot, peer):
        j, q = divmod(p, rows_dev)
        recv_sem = halo_recv.at[kind, j] if kind == TO_RELAY else piece_recv.at[kind, p]
        return pltpu.make_async_remote_copy(
            src_ref=windows[j].at[rows_dev * from_slot + q], dst_ref=windows[j].at[rows_dev * to_slot + q],
            send_sem=halo_send.at[kind, j], recv_sem=recv_sem, device_id={"row": peer}, device_id_type=MESH)

    y_way = (HALO, HALO - 2 * sign_y, me + 2 * sign_y)
    core_way = (HALO, HALO - sign_c, me + sign_c)
    z_way = (HALO + 2 * sign_y, HALO - 2 * sign_y, z_to)
    relay_way = (HALO + 2 * sign_c, HALO + sign_c, me + sign_c)
    relay_sends = jnp.logical_or(sign_y == sign_c, z_comes)
    relay_comes = jnp.logical_or(sign_y != sign_c, z_comes)
    first_block = (me - HALO) * rows_dev
    pieces = CHUNKS * rows_dev

    def own(j):
        all_rows(j).wait_recv()
        own_rows[j].wait()
        rows = arrived[j][...].reshape(n * cap, wide)
        for q in range(rows_dev):
            place = slice(q * block, (q + 1) * block)
            injected = jnp.dot(landing[place], rows, preferred_element_type=F32)
            before_it = base[place, j * wide:(j + 1) * wide].astype(F32)
            windows[j][HALO * rows_dev + q] = (before_it + injected).astype(BF16)
            piece_copy(TO_Y, j * rows_dev + q, *y_way).start()
        halo_copy(TO_CORE, j, *core_way).start()

    def y_arrives(p):
        slot = HALO + 2 * sign_y
        piece_copy(TO_Y, p, slot, slot, me + 2 * sign_y).wait_recv()

        @pl.when(z_sends)
        def _():
            piece_copy(TO_Z, p, *z_way).start()

        @pl.when(sign_y == sign_c)
        def _():
            piece_copy(TO_RELAY, p, *relay_way).start()

    def z_arrives(p):
        slot = HALO - 2 * sign_y

        @pl.when(z_comes)
        def _():
            piece_copy(TO_Z, p, slot, slot, me + 2 * sign_y).wait_recv()

        @pl.when(jnp.logical_and(z_comes, sign_y != sign_c))
        def _():
            piece_copy(TO_RELAY, p, *relay_way).start()

    def window_complete(j):
        halo_copy(TO_CORE, j, HALO + sign_c, HALO + sign_c, me + sign_c).wait_recv()

        @pl.when(relay_comes)
        def _():
            halo_copy(TO_RELAY, j, HALO - sign_c, HALO - sign_c, me + sign_c).wait_recv()

    def compute(j, r):
        total = jnp.zeros((block, wide), F32)
        for k in range(stored):
            place = jnp.clip(cols_ref[r, k] - first_block, 0, windows[j].shape[0] - 1)
            total = total + jnp.dot(blocks[r, k], windows[j][place], preferred_element_type=F32)
        results[j][r * block:(r + 1) * block] = total.astype(BF16)

    def store(j):
        return pltpu.make_async_copy(results[j], out_hbm.at[:, pl.ds(j * wide, wide)], store_sem.at[j])

    for j in range(CHUNKS - 2):
        if j < 2:
            own(j)
        next_rows(j + 2)
    z_lag, lag = 2, rows_dev + 2
    for p in range(pieces + lag):
        if p < pieces:
            y_arrives(p)
            if p % rows_dev == 0 and p // rows_dev + 2 < CHUNKS:
                own(p // rows_dev + 2)
        if 0 <= p - z_lag < pieces:
            z_arrives(p - z_lag)
        if p == lag:
            load_cols.wait()
            load_blocks.wait()
            all_tags().wait_send()
            all_rows(CHUNKS - 1).wait_send()
        if p >= lag:
            j, r = divmod(p - lag, rows_dev)
            if r == 0:
                window_complete(j)
            compute(j, r)
            if r == rows_dev - 1:
                store(j).start()

    for j in range(CHUNKS):
        halo_copy(TO_Y, j, *y_way).wait_send()
        halo_copy(TO_CORE, j, *core_way).wait_send()

        @pl.when(z_sends)
        def _():
            halo_copy(TO_Z, j, *z_way).wait_send()

        @pl.when(relay_sends)
        def _():
            halo_copy(TO_RELAY, j, *relay_way).wait_send()

        store(j).wait()


def shards(base_currents, term_rows, term_owner, term_slot, inductance, block_cols):
    n = lax.axis_size("row")
    seg_dev, width = base_currents.shape
    count = term_rows.shape[0]
    rows_dev, stored, block, _ = inductance.shape
    cap = max(16, 2 * count // n)
    wide = width // CHUNKS
    span = (2 * HALO + 1) * rows_dev
    hbm = pl.BlockSpec(memory_space=pl.ANY)
    dma = pltpu.SemaphoreType.DMA
    return pl.pallas_call(
        functools.partial(kernel, n, cap),
        out_shape=jax.ShapeDtypeStruct((seg_dev, width), BF16),
        in_specs=[hbm] * 6,
        out_specs=hbm,
        scratch_shapes=(
            [pltpu.VMEM((span, block, wide), BF16)] * CHUNKS
            + [pltpu.VMEM((n, cap, wide), BF16)] * CHUNKS
            + [pltpu.VMEM((n, cap, wide), BF16)] * CHUNKS
            + [pltpu.VMEM((seg_dev, wide), BF16)] * CHUNKS
            + [
                pltpu.SMEM(block_cols.shape, jnp.int32),
                pltpu.VMEM((1, count), jnp.int32),
                pltpu.VMEM((1, count), jnp.int32),
                pltpu.VMEM((count, width), BF16),
                pltpu.VMEM((seg_dev, width), BF16),
                pltpu.VMEM(inductance.shape, BF16),
                pltpu.VMEM((seg_dev, n * cap), BF16),
                pltpu.VMEM((n, 8, LANES), jnp.int32),
                pltpu.VMEM((n, 8, LANES), jnp.int32),
                dma((6,)),
                dma((CHUNKS + 1,)),
                dma((CHUNKS,)),
                dma((CHUNKS,)),
                dma((CHUNKS,)),
                dma((2,)),
                dma((4, CHUNKS)),
                dma((4, CHUNKS)),
                dma((2, CHUNKS * rows_dev)),
            ]
        ),
        compiler_params=pltpu.CompilerParams(
            collective_id=0, has_side_effects=True, vmem_limit_bytes=60 * 2**20
        ),
        cost_estimate=pl.CostEstimate(
            flops=2 * rows_dev * stored * block * block * width,
            bytes_accessed=2 * (inductance.size + 2 * base_currents.size + term_rows.size),
            transcendentals=0,
        ),
    )(block_cols, term_owner.reshape(1, count), term_slot.reshape(1, count), term_rows, base_currents, inductance)


def solution(mesh):
    placed = (
        P(("group", "row"), None),
        P(("group", "row"), None),
        P(("group", "row"), None),
        P(("group", "row"), None),
        P("row", None, None, None),
        P("row", None),
    )
    return jax.shard_map(
        shards, mesh=mesh, in_specs=placed, out_specs=P(("group", "row"), None), check_vma=False
    )
```
